32 devices in a mesh: groups: 2 (over x), head: 16 (over z, y, core).
Axes of the slice: x: 2, y: 2, z: 4, core: 2. Of those that a mesh axis runs over, the one named last changes fastest.
Arguments:
- inputs: bfloat16 [6, 16, 8192], P('groups', None, 'head'), parts along dimension 0, may hold values from -6 to 6
- w_query: bfloat16 [8192, 8192], P(None, 'head'), may hold values from -0.0625 to 0.0625
- w_keyval: bfloat16 [8192, 2048], P(None, 'head'), may hold values from -0.21875 to 0.21875
- w_out: bfloat16 [8192, 8192], P('head'), may hold values from -0.0625 to 0.0625
- prefix_keys: bfloat16 [24576, 1024], P(('groups', 'head')), parts along dimension 0, may hold values from -136 to 136
- prefix_values: bfloat16 [24576, 1024], P(('groups', 'head')), parts along dimension 0, may hold values from -24 to 24
- suffix_keys: bfloat16 [256, 64, 128], P(('groups', 'head')), parts along dimension 0, may hold values from -20 to 20
- suffix_values: bfloat16 [256, 64, 128], P(('groups', 'head')), parts along dimension 0, may hold values from -24 to 24
- page_table: int32 [32, 4], P('groups'), parts along dimension 0, may hold values from 0 to 3, each once within a row
- suffix_len: int32 [32], P('groups'), parts along dimension 0, may hold values from 1 to 64, 640 in all
- parents: int32 [6, 16], P('groups'), parts along dimension 0, may hold values from 0 to 15
Outputs:
- outputs: bfloat16 [6, 16, 8192], P('groups', None, 'head'), parts along dimension 0
The draws below stay inside these ranges and needn't reach their ends.
There are 2 independent parts, one for each index of `groups`. The reference program is written for one: setup_inputs(seed, part) draws one part's arguments, and reference() takes and returns one part's arrays. A program takes and returns all parts, laid end to end along the dimension named above; an argument that names none is the same for every part. Nothing has to cross between parts.
Inputs may be any that keep to these rules, and one draw needn't show every extreme that they name: `page_table`: each row is a permutation of the 4 pages of that beam. `suffix_len`: the largest length is 64.
All inputs are finite; a program needn't handle non-finite values.
Results may differ from the reference program's by a relative error of at most 0.006.
The reference program's roundings to bfloat16 on the way count: a program that leaves them out, or rounds other values in their place, can miss the bound.
Values may be sent and summed in bfloat16 or wider, within the bound.
A program may use at most 128 MiB of HBM per device.

```python
import math
import jax
import jax.numpy as jnp
import numpy as np
from jax import lax

D = 8192
H = 64
KVH = 8
HDIM = 128
B = 16
STEPS = 3
PAGE = 16
PAGES = 4
PREFIX = 12288


def draw_prefix_keys(key, part):
    key = jax.random.fold_in(key, 11)
    key_scale, key_base = jax.random.split(key, 2)
    spread = jnp.exp(jax.random.uniform(key_scale, (PREFIX, 1), jnp.float32, math.log(0.5), math.log(3.0)))
    values = jax.random.truncated_normal(key_base, -4.0, 4.0, (PREFIX, KVH * HDIM), jnp.float32)
    return (values * spread).astype(jnp.bfloat16)


def plant(values, stream_key, least, top_value):
    extent = values.shape
    index_at = [jax.random.randint(jax.random.fold_in(stream_key, axis), (), 0, extent[axis]) for axis in range(len(extent))]
    values = values.at[tuple(index_at)].set(least)
    longest = extent.index(max(extent))
    index_at[longest] = (index_at[longest] + 1) % extent[longest]
    return values.at[tuple(index_at)].set(top_value)


def levels(own_key, dims, cuts, least, high):
    def one(dim, shards_of):
        heights = jax.random.uniform(jax.random.fold_in(jax.random.fold_in(own_key, 6), dim), (shards_of,), jnp.float32, least / len(cuts), high / len(cuts))
        return jnp.repeat(jnp.exp(heights), dims[dim] // shards_of).reshape((-1,) + (1,) * (len(dims) - dim - 1))

    loudness = one(*cuts[0])
    for cut in cuts[1:]:
        loudness = loudness * one(*cut)
    return loudness


def rank_table(count, skew):
    weights = [(1 << 20) // math.isqrt(standing ** skew) + 1 for standing in range(1, count + 1)]
    scale = 1 + sum(weights) // (1 << 30)
    return np.cumsum(np.array([max(1, weight // scale) for weight in weights]))


def ranked(rng, shape, amount, skew):
    table = rank_table(amount, skew)
    pick = jax.random.randint(jax.random.fold_in(rng, 1), shape, 0, int(table[amount - 1]))
    standing = jnp.searchsorted(jnp.asarray(table, jnp.int32), pick, side="right")
    return jax.random.permutation(jax.random.fold_in(rng, 2), amount)[standing].astype(jnp.int32)


def length_profile(count, total, most, skew):
    weights = [(1 << 20) // math.isqrt(rank ** skew) + 1 for rank in range(2, count + 1)]
    spare, given = total - most - (count - 1), [1] * (count - 1)
    while spare > 0:
        free = [i for i in range(count - 1) if given[i] < most]
        mass, budget = sum([weights[i] for i in free]), spare
        for i in free:
            more = min(most - given[i], max(1, budget * weights[i] // mass), spare)
            given[i] = given[i] + more
            spare = spare - more
    return np.array([most] + given)


def uneven_parts(own_key, count, total, most, skew):
    if count == 2:
        one = jax.random.randint(own_key, (), max(1, total - most), min(most, total - 1) + 1)
        return jnp.stack([one, total - one])
    sizes = jnp.asarray(length_profile(count, total, most, skew), jnp.int32)
    twos = (count - 1) // 2
    source_of, sink = sizes[1:1 + 2 * twos:2], sizes[2:2 + 2 * twos:2]
    room = jnp.minimum(source_of - 1, most - sink)
    moved = jax.random.randint(jax.random.fold_in(own_key, 1), (twos,), 0, 1 << 20) % (room + 1)
    sizes = sizes.at[1:1 + 2 * twos:2].set(source_of - moved).at[2:2 + 2 * twos:2].set(sink + moved)
    return sizes[jax.random.permutation(jax.random.fold_in(own_key, 2), count)]


def gaussian(stream_key, shape, width, bound, cuts=(), kind=jnp.bfloat16):
    values = jax.random.normal(stream_key, shape, jnp.float32) * width
    if len(cuts) > 0:
        values = levels(stream_key, shape, cuts, -0.22, 0.18) * values
    return jnp.clip(values, min=-bound, max=bound).astype(kind)


def setup_inputs(seed: int = 0, part: int = 0) -> dict:
    arg_keys = jax.random.split(jax.random.key(seed), 12)
    part_splits = jax.random.split(jax.random.fold_in(arg_keys[11], part), 12)
    return {
        "inputs": gaussian(part_splits[0], (STEPS, B, D), 1.0, 6.0, ((2, 16),)),
        "w_query": gaussian(arg_keys[1], (D, H * HDIM), D ** -0.5, 0.0625, ((1, 16),)),
        "w_keyval": gaussian(arg_keys[2], (D, 2 * KVH * HDIM), (D // 12) ** -0.5, 0.21875, ((1, 16),)),
        "w_out": gaussian(arg_keys[3], (H * HDIM, D), (H * HDIM) ** -0.5, 0.0625, ((0, 16),)),
        "prefix_keys": draw_prefix_keys(jax.random.fold_in(jax.random.fold_in(arg_keys[11], part), 71), part),
        "prefix_values": gaussian(part_splits[5], (PREFIX, KVH * HDIM), 4.0, 24.0, ((0, 16),)),
        "suffix_keys": gaussian(part_splits[6], (B * KVH, PAGES * PAGE, HDIM), 3.5, 20.0, ((0, 16),)),
        "suffix_values": gaussian(part_splits[7], (B * KVH, PAGES * PAGE, HDIM), 4.0, 24.0, ((0, 16),)),
        "page_table": jax.vmap(lambda own: jax.random.permutation(own, PAGES))(jax.random.split(part_splits[8], B)).reshape((B, PAGES)).astype(jnp.int32),
        "suffix_len": uneven_parts(part_splits[9], B, B * PAGES * PAGE * 5 // 8, PAGES * PAGE, 2).astype(jnp.int32),
        "parents": plant(ranked(part_splits[10], (STEPS, B), B, 2), jax.random.fold_in(part_splits[10], 3), 0, B - 1).astype(jnp.int32),
    }


def lookup(lookup_table, indices):
    row_count = lookup_table.shape[0]
    matches = indices[:, None] == jnp.arange(row_count, dtype=jnp.int32)[None, :]
    return lax.optimization_barrier(jnp.sum(jnp.where(matches, lookup_table[None, :], 0), axis=1)).astype(jnp.int32)

def slot_valid(page_table, suffix_len):
    beam_count, page_count = page_table.shape
    page_ids = jnp.arange(page_count, dtype=jnp.int32)
    matches = page_table[:, :, None] == page_ids[None, None, :]
    logical = lax.optimization_barrier(jnp.sum(jnp.where(matches, page_ids[None, :, None], 0), axis=1)).astype(jnp.int32)
    position = logical[:, :, None] * PAGE + jnp.arange(PAGE, dtype=jnp.int32)[None, None, :]
    inside = position.reshape(beam_count, page_count * PAGE) < suffix_len[:, None]
    return jnp.where(inside, 1, 0).astype(jnp.int32)

def rounded(values):
    return lax.optimization_barrier(values.astype(jnp.bfloat16)).astype(jnp.float32)

def reference(inputs, w_query, w_keyval, w_out, prefix_keys, prefix_values, suffix_keys, suffix_values, page_table, suffix_len, parents):
    group_size = H // KVH
    slot_count = PAGES * PAGE
    score_scale = 1.0 / math.sqrt(HDIM)
    valid_orig = slot_valid(page_table, suffix_len)
    cache_keys = suffix_keys.reshape(B, KVH, slot_count, HDIM)
    cache_values = suffix_values.reshape(B, KVH, slot_count, HDIM)
    pre_keys = prefix_keys.reshape(PREFIX, KVH, HDIM)
    pre_values = prefix_values.reshape(PREFIX, KVH, HDIM)
    keyval_list = []
    results = []
    for step_index in range(STEPS):
        tokens = inputs[step_index]
        queries = jnp.dot(tokens, w_query, preferred_element_type=jnp.float32).astype(jnp.bfloat16)
        keyvals = jnp.dot(tokens, w_keyval, preferred_element_type=jnp.float32).astype(jnp.bfloat16)
        keyval_list.append(keyvals)
        lineage = [None] * (step_index + 1)
        current = jnp.arange(B, dtype=jnp.int32)
        lineage[step_index] = current
        for later_step in range(step_index, 0, -1):
            current = lookup(parents[later_step], current)
            lineage[later_step - 1] = current
        ancestor = lookup(parents[0], current)
        fresh_rows = jnp.stack([keyval_list[earlier][lineage[earlier]] for earlier in range(step_index + 1)])
        fresh_keys = fresh_rows[:, :, :KVH * HDIM].reshape(step_index + 1, B, KVH, HDIM)
        fresh_values = fresh_rows[:, :, KVH * HDIM:].reshape(step_index + 1, B, KVH, HDIM)
        query_heads = queries.reshape(B, KVH, group_size, HDIM).astype(jnp.float32)
        ancestor_ok = valid_orig[ancestor] > 0
        heads_out = []
        for kv_head in range(KVH):
            query_block = query_heads[:, kv_head]
            score_pre = jnp.einsum('bgd,pd->bgp', query_block, pre_keys[:, kv_head].astype(jnp.float32)) * score_scale
            anc_keys = cache_keys[ancestor, kv_head].astype(jnp.float32)
            anc_values = cache_values[ancestor, kv_head].astype(jnp.float32)
            score_suf = jnp.einsum('bgd,bsd->bgs', query_block, anc_keys) * score_scale
            score_suf = jnp.where(ancestor_ok[:, None, :], score_suf, -jnp.inf)
            score_new = jnp.einsum('bgd,sbd->bgs', query_block, fresh_keys[:, :, kv_head].astype(jnp.float32)) * score_scale
            largest = jnp.maximum(jnp.maximum(lax.optimization_barrier(jnp.max(score_pre, axis=2)), lax.optimization_barrier(jnp.max(score_suf, axis=2))), lax.optimization_barrier(jnp.max(score_new, axis=2)))
            weight_pre = jnp.exp(score_pre - largest[..., None])
            weight_suf = jnp.exp(score_suf - largest[..., None])
            weight_new = jnp.exp(score_new - largest[..., None])
            total = lax.optimization_barrier(jnp.sum(weight_pre, axis=2)) + lax.optimization_barrier(jnp.sum(weight_suf, axis=2)) + lax.optimization_barrier(jnp.sum(weight_new, axis=2))
            numerator = jnp.einsum('bgp,pd->bgd', rounded(weight_pre), pre_values[:, kv_head].astype(jnp.float32))
            numerator = numerator + jnp.einsum('bgs,bsd->bgd', rounded(weight_suf), anc_values)
            numerator = numerator + jnp.einsum('bgs,sbd->bgd', rounded(weight_new), fresh_values[:, :, kv_head].astype(jnp.float32))
            heads_out.append(numerator / total[..., None])
        attended = jnp.stack(heads_out, axis=1).reshape(B, H * HDIM).astype(jnp.bfloat16)
        results.append(jnp.dot(attended, w_out, preferred_element_type=jnp.float32).astype(jnp.bfloat16))
    return jnp.stack(results)
```

```python
import functools
import math

import jax
import jax.numpy as jnp
from jax import lax
from jax.experimental import pallas as pl
from jax.experimental.pallas import tpu as pltpu
from jax.sharding import PartitionSpec as P

NEG = float("-inf")


def lookup(lookup_table, indices):
    row_count = lookup_table.shape[0]
    matches = indices[:, None] == jnp.arange(row_count, dtype=jnp.int32)[None, :]
    return jnp.sum(jnp.where(matches, lookup_table[None, :], 0), axis=1)


def reverse_bits(index, bits):
    total = 0
    for i in range(bits):
        total = total + ((index // (1 << i)) % 2) * (1 << (bits - 1 - i))
    return total


def masks(page_table, suffix_len, parents, my_beam, slots):
    steps, beams = parents.shape
    page_count = page_table.shape[1]
    page_size = slots // page_count
    beam_ids = jnp.arange(beams, dtype=jnp.int32)
    mine = beam_ids == my_beam
    own_pages = jnp.sum(jnp.where(mine[:, None], page_table, 0), axis=0)
    own_len = jnp.sum(jnp.where(mine, suffix_len, 0))
    page_ids = jnp.arange(page_count, dtype=jnp.int32)
    logical = jnp.sum(
        jnp.where(own_pages[:, None] == page_ids[None, :], page_ids[:, None], 0), axis=0
    )
    place = logical[:, None] * page_size + jnp.arange(page_size, dtype=jnp.int32)[None, :]
    slot_ok = place.reshape(slots) < own_len
    suffix_rows, fresh_rows = [], []
    for step in range(steps):
        current = beam_ids
        hits = [None] * steps
        hits[step] = current
        for later in range(step, 0, -1):
            current = lookup(parents[later], current)
            hits[later - 1] = current
        ancestor = lookup(parents[0], current)
        suffix_rows.append((ancestor == my_beam)[:, None] & slot_ok[None, :])
        fresh_rows.append(
            jnp.concatenate(
                [
                    jnp.zeros((beams, beams), bool)
                    if hit is None
                    else hit[:, None] == beam_ids[None, :]
                    for hit in hits
                ],
                axis=1,
            )
        )
    suffix_ok = jnp.concatenate(suffix_rows, axis=0)
    fresh_ok = jnp.concatenate(fresh_rows, axis=0)
    suffix_ok = jnp.pad(suffix_ok, ((0, 0), (0, 128 - suffix_ok.shape[1])))
    fresh_ok = jnp.pad(fresh_ok, ((0, 0), (0, 128 - fresh_ok.shape[1])))
    return jnp.where(jnp.stack([suffix_ok, fresh_ok]), 0.0, NEG).astype(jnp.float32)


def kernel(
    n,
    x_ref,
    sk_ref,
    sv_ref,
    mask_ref,
    wq_hbm,
    wkv_hbm,
    wo_hbm,
    pk_hbm,
    pv_hbm,
    out_ref,
    xg,
    qg,
    kvg,
    wq,
    wkv,
    wo,
    pk,
    pv,
    ske,
    sve,
    scores,
    fresh,
    maxes,
    max_in,
    acc,
    acc_in,
    y,
    y_in,
    proj_q,
    proj_kv,
    load_sem,
    send_sem,
    recv_sem,
):
    bits = n.bit_length() - 1
    me = lax.axis_index("head")
    pme = reverse_bits(me, bits)
    tokens, dl = x_ref.shape
    width_q = wq.shape[1]
    width_kv = wkv.shape[1]
    hd = 128
    hq = width_q // hd
    rows = hq * tokens
    own_rows, slots = sk_ref.shape[0], sk_ref.shape[1]
    kv_heads = pk.shape[1] // hd
    group_size = hq * n // kv_heads
    pre = pk.shape[0]
    scale = 1.0 / math.sqrt(hd)
    first_kv = me * own_rows % kv_heads
    blocks = -(-rows // 128)
    f32, bf16 = jnp.float32, jnp.bfloat16

    loads = [
        pltpu.make_async_copy(src, dst, load_sem.at[i])
        for i, (src, dst) in enumerate(
            ((wq_hbm, wq), (wkv_hbm, wkv), (pk_hbm, pk), (pv_hbm, pv), (wo_hbm, wo))
        )
    ]
    for load in loads:
        load.start()

    def bit(i):
        return (me // (1 << i)) % 2

    def partner(i):
        return me + (1 - 2 * bit(i)) * (1 << i)

    barrier = pltpu.get_barrier_semaphore()
    for i in range(bits):
        pl.semaphore_signal(
            barrier, inc=1, device_id={"head": partner(i)}, device_id_type=pl.DeviceIdType.MESH
        )

    xg[pme] = x_ref[...]
    for r in range(own_rows):
        zeros = jnp.zeros((hd - slots, hd), bf16)
        ske[r, :slots] = sk_ref[r]
        ske[r, slots:] = zeros
        sve[r, :slots] = sv_ref[r]
        sve[r, slots:] = zeros
    proj_q[...] = jnp.zeros_like(proj_q)
    proj_kv[...] = jnp.zeros_like(proj_kv)
    pl.semaphore_wait(barrier, bits)

    def send(src, dst, phase, step, i):
        copy = pltpu.make_async_remote_copy(
            src_ref=src,
            dst_ref=dst,
            send_sem=send_sem.at[phase, step],
            recv_sem=recv_sem.at[phase, step],
            device_id={"head": partner(i)},
            device_id_type=pl.DeviceIdType.MESH,
        )
        copy.start()
        return copy

    def gather_step(buf, phase, k):
        count = 1 << k
        base = (pme // count) * count
        part = buf.at[pl.ds(base, count)]
        return send(part, part, phase, k, bits - 1 - k)

    def gather_range(k):
        count = 1 << k
        base = (pme // count) * count
        return base + (1 - 2 * bit(bits - 1 - k)) * count, count

    def each(start, count, body):
        def run(i, carry):
            body(start + i)
            return carry

        lax.fori_loop(0, count, run, 0)

    def project(p):
        j = reverse_bits(p, bits)
        at = pl.ds(pl.multiple_of(j * dl, dl), dl)
        block = xg[p]
        proj_q[...] += jnp.dot(block, wq[at, :], preferred_element_type=f32)
        proj_kv[...] += jnp.dot(block, wkv[at, :], preferred_element_type=f32)

    start, count = pme, 1
    for k in range(bits):
        copy = gather_step(xg, 0, k)
        if k == 0:
            loads[0].wait()
            loads[1].wait()
        each(start, count, project)
        copy.wait()
        start, count = gather_range(k)
    each(start, count, project)

    for h in range(hq):
        qg[pme, h * tokens : (h + 1) * tokens, :] = proj_q[:, h * hd : (h + 1) * hd].astype(bf16)
    kvg[pme] = proj_kv[...].astype(bf16)

    row_id = lax.broadcasted_iota(jnp.int32, (rows, 128), 0)
    lane_id = lax.broadcasted_iota(jnp.int32, (rows, 128), 1)
    eye = row_id % 128 == lane_id

    def to_rows(column, fill, reduce):
        spread = jnp.where(eye, jnp.broadcast_to(column, (rows, 128)), fill)
        return [
            reduce(spread[i * 128 : min(rows, (i + 1) * 128)], axis=0, keepdims=True)
            for i in range(blocks)
        ]

    def to_column(parts, fill, reduce):
        return jnp.concatenate(
            [
                reduce(
                    jnp.where(
                        eye[: min(128, rows - i * 128)],
                        jnp.broadcast_to(part, (min(128, rows - i * 128), 128)),
                        fill,
                    ),
                    axis=1,
                    keepdims=True,
                )
                for i, part in enumerate(parts)
            ],
            axis=0,
        )

    def heads_of(p):
        kv = reverse_bits(p, bits) * hq // group_size
        off = kv - first_kv
        return kv, off

    suffix_mask = jnp.concatenate([mask_ref[0]] * hq, axis=0)

    def clip(off):
        return jnp.minimum(jnp.maximum(off, 0), own_rows - 1)

    def score(p):
        kv, off = heads_of(p)
        q = qg[p]
        keys = pk[:, pl.ds(pl.multiple_of(kv * hd, hd), hd)]
        nt = (((1,), (1,)), ((), ()))
        s = lax.dot_general(q, keys, nt, preferred_element_type=f32) * scale
        scores[p, :, :pre] = s
        hit = jnp.where((off >= 0) & (off < own_rows), 0.0, NEG)
        e = lax.dot_general(q, ske[clip(off)], nt, preferred_element_type=f32) * scale
        e = e + suffix_mask + hit
        scores[p, :, pre:] = e
        m = jnp.maximum(jnp.max(s, axis=1, keepdims=True), jnp.max(e, axis=1, keepdims=True))
        for i, part in enumerate(to_rows(m, NEG, jnp.max)):
            maxes[0, p, i : i + 1, :] = part

    start, count = pme, 1
    for k in range(bits):
        copies = (gather_step(qg, 1, k), gather_step(kvg, 2, k))
        if k == 0:
            loads[2].wait()
        each(start, count, score)
        for copy in copies:
            copy.wait()
        start, count = gather_range(k)
    each(start, count, score)

    own_kv = me * hq // group_size
    pieces = hd // width_kv if width_kv < hd else 1

    def fresh_block(column):
        if width_kv >= hd:
            j = column * hd // width_kv
            return kvg[reverse_bits(j, bits)]
        j = column * pieces
        return jnp.concatenate([kvg[reverse_bits(j + i, bits)] for i in range(pieces)], axis=1)

    fresh_keys = fresh_block(own_kv)
    fresh_values = fresh_block(own_kv + kv_heads)
    pad = jnp.zeros((hd - tokens, hd), bf16)
    fresh_keys = jnp.concatenate([fresh_keys, pad], axis=0)
    fresh_values = jnp.concatenate([fresh_values, pad], axis=0)
    f = lax.dot_general(
        qg[pme], fresh_keys, (((1,), (1,)), ((), ())), preferred_element_type=f32
    )
    f = f * scale + jnp.concatenate([mask_ref[1]] * hq, axis=0)
    fresh[...] = f
    for i, part in enumerate(to_rows(jnp.max(f, axis=1, keepdims=True), NEG, jnp.max)):
        maxes[0, pme, i : i + 1, :] = jnp.maximum(maxes[0, pme, i : i + 1, :], part)

    for k in range(bits):
        send(maxes.at[k], max_in.at[k], 3, k, k).wait()
        maxes[k + 1] = jnp.maximum(maxes[k], max_in[k])

    loads[3].wait()

    def largest(p):
        return to_column(
            [maxes[bits, p, i : i + 1, :] for i in range(blocks)], NEG, jnp.max
        )

    def put_totals(p, column):
        parts = to_rows(column, 0.0, jnp.sum)
        parts.append(jnp.zeros((8 - blocks, 128), f32))
        acc[p, rows:, :] = jnp.concatenate(parts, axis=0)

    def weigh(p):
        kv, off = heads_of(p)
        w = jnp.exp(scores[p] - largest(p))
        values = pv[:, pl.ds(pl.multiple_of(kv * hd, hd), hd)]
        wb = w.astype(bf16)
        acc[p, :rows, :] = jnp.dot(
            wb[:, :pre], values, preferred_element_type=f32
        ) + jnp.dot(wb[:, pre:], sve[clip(off)], preferred_element_type=f32)
        put_totals(p, jnp.sum(w, axis=1, keepdims=True))

    def scatter_sum(buf, buf_in, phase, fill, own_extra):
        offset = 0
        count = n // 2
        for k in range(bits):
            keep = (pme // count) * count
            away = keep + (1 - 2 * bit(k)) * count
            if k == 0:
                each(away, count, fill)
            else:
                before = offset - 2 * count
                prior = (pme // (2 * count)) * (2 * count)

                def add(p):
                    buf[p] += buf_in[before + p - prior]

                each(away, count, add)
            copy = send(
                buf.at[pl.ds(away, count)], buf_in.at[pl.ds(offset, count)], phase, k, k
            )
            if k == 0:
                each(keep, count, fill)
                own_extra()
            else:
                each(keep, count, add)
            copy.wait()
            offset += count
            count //= 2
        return buf[pme] + buf_in[offset - 1]

    def add_fresh():
        w = jnp.exp(fresh[...] - largest(pme))
        acc[pme, :rows, :] += jnp.dot(
            w.astype(bf16), fresh_values, preferred_element_type=f32
        )
        parts = to_rows(jnp.sum(w, axis=1, keepdims=True), 0.0, jnp.sum)
        parts.append(jnp.zeros((8 - blocks, 128), f32))
        acc[pme, rows:, :] += jnp.concatenate(parts, axis=0)

    total = scatter_sum(acc, acc_in, 4, weigh, add_fresh)
    column = to_column([total[rows + i : rows + i + 1] for i in range(blocks)], 0.0, jnp.sum)
    attended = (total[:rows] / column).astype(bf16)
    attended = jnp.concatenate(
        [attended[h * tokens : (h + 1) * tokens] for h in range(hq)], axis=1
    )
    loads[4].wait()

    def out_block(p):
        j = reverse_bits(p, bits)
        columns = wo[:, pl.ds(pl.multiple_of(j * dl, dl), dl)]
        y[p] = jnp.dot(attended, columns, preferred_element_type=f32)

    result = scatter_sum(y, y_in, 5, out_block, lambda: None)
    out_ref[...] = result.astype(bf16)


def local(
    inputs,
    w_query,
    w_keyval,
    w_out,
    prefix_keys,
    prefix_values,
    suffix_keys,
    suffix_values,
    page_table,
    suffix_len,
    parents,
):
    n = lax.axis_size("head")
    bits = n.bit_length() - 1
    me = lax.axis_index("head")
    steps, beams, dl = inputs.shape
    tokens = steps * beams
    own_rows, slots, hd = suffix_keys.shape
    kv_heads = prefix_keys.shape[1] // hd
    my_beam = me * own_rows // kv_heads
    width_q, width_kv = w_query.shape[1], w_keyval.shape[1]
    rows = width_q // hd * tokens
    blocks = -(-rows // 128)
    pre = prefix_keys.shape[0]
    mask = masks(page_table, suffix_len, parents, my_beam, slots)
    bf16, f32 = jnp.bfloat16, jnp.float32
    vmem = pl.BlockSpec(memory_space=pltpu.VMEM)
    hbm = pl.BlockSpec(memory_space=pl.ANY)
    out = pl.pallas_call(
        functools.partial(kernel, n),
        out_shape=jax.ShapeDtypeStruct((tokens, dl), bf16),
        in_specs=[vmem] * 4 + [hbm] * 5,
        out_specs=vmem,
        scratch_shapes=[
            pltpu.VMEM((n, tokens, dl), bf16),
            pltpu.VMEM((n, rows, hd), bf16),
            pltpu.VMEM((n, tokens, width_kv), bf16),
            pltpu.VMEM(w_query.shape, bf16),
            pltpu.VMEM(w_keyval.shape, bf16),
            pltpu.VMEM(w_out.shape, bf16),
            pltpu.VMEM(prefix_keys.shape, bf16),
            pltpu.VMEM(prefix_values.shape, bf16),
            pltpu.VMEM((own_rows, hd, hd), bf16),
            pltpu.VMEM((own_rows, hd, hd), bf16),
            pltpu.VMEM((n, rows, pre + hd), f32),
            pltpu.VMEM((rows, hd), f32),
            pltpu.VMEM((bits + 1, n, blocks, 128), f32),
            pltpu.VMEM((bits, n, blocks, 128), f32),
            pltpu.VMEM((n, rows + 8, hd), f32),
            pltpu.VMEM((n - 1, rows + 8, hd), f32),
            pltpu.VMEM((n, tokens, dl), f32),
            pltpu.VMEM((n - 1, tokens, dl), f32),
            pltpu.VMEM((tokens, width_q), f32),
            pltpu.VMEM((tokens, width_kv), f32),
            pltpu.SemaphoreType.DMA((5,)),
            pltpu.SemaphoreType.DMA((6, bits)),
            pltpu.SemaphoreType.DMA((6, bits)),
        ],
        compiler_params=pltpu.CompilerParams(
            collective_id=0, has_side_effects=True, vmem_limit_bytes=56 * 1024 * 1024
        ),
    )(
        inputs.reshape(tokens, dl),
        suffix_keys,
        suffix_values,
        mask,
        w_query,
        w_keyval,
        w_out,
        prefix_keys,
        prefix_values,
    )
    return out.reshape(steps, beams, dl)


def solution(mesh):
    return jax.shard_map(
        local,
        mesh=mesh,
        in_specs=(
            P("groups", None, "head"),
            P(None, "head"),
            P(None, "head"),
            P("head", None),
            P(("groups", "head"), None),
            P(("groups", "head"), None),
            P(("groups", "head"), None, None),
            P(("groups", "head"), None, None),
            P("groups", None),
            P("groups"),
            P("groups", None),
        ),
        out_specs=P("groups", None, "head"),
        check_vma=False,
    )
```

```python
import functools
import math

import jax
import jax.numpy as jnp
from jax import lax
from jax.experimental import pallas as pl
from jax.experimental.pallas import tpu as pltpu
from jax.sharding import PartitionSpec as P

NEG = float("-inf")


def masks(table_ref, len_ref, parents_ref, my_beam, slots, steps):
    i32 = jnp.int32
    beams, page_count = table_ref.shape
    page_size = slots // page_count
    lane = lax.broadcasted_iota(i32, (beams, 128), 1)
    row = lax.broadcasted_iota(i32, (beams, 128), 0)
    own_pages = jnp.where(
        lax.broadcasted_iota(i32, (beams, page_count), 0) == my_beam, table_ref[...], 0
    )
    page_of = jnp.zeros((beams, 128), i32)
    for page in range(1, page_count):
        page_of = page_of + jnp.where(lane >= page * page_size, 1, 0)
    logical = jnp.zeros((beams, 128), i32)
    for page in range(1, page_count):
        physical = jnp.sum(own_pages[:, page : page + 1], axis=0, keepdims=True)
        logical = logical + jnp.where(page_of == physical, page, 0)
    beam_lane = lax.broadcasted_iota(i32, (1, beams), 1)
    own_len = jnp.sum(
        jnp.where(beam_lane == my_beam, len_ref[...], 0), axis=1, keepdims=True
    )
    place = logical * page_size + lane - page_of * page_size
    slot_ok = jnp.where((place < own_len) & (lane < slots), 1, 0)
    square_lane = lax.broadcasted_iota(i32, (beams, beams), 1)
    square_row = lax.broadcasted_iota(i32, (beams, beams), 0)

    def lookup(step, column):
        table = jnp.broadcast_to(parents_ref[step : step + 1, :], (beams, beams))
        return jnp.sum(jnp.where(square_lane == column, table, 0), axis=1, keepdims=True)

    first = jnp.sum(jnp.where(square_lane == square_row, square_lane, 0), axis=1, keepdims=True)
    suffix_rows, fresh_rows = [], []
    for step in range(steps):
        current = first
        fresh_ok = jnp.where(lane == current + step * beams, 1, 0)
        for later in range(step, 0, -1):
            current = lookup(later, current)
            fresh_ok = fresh_ok + jnp.where(lane == current + (later - 1) * beams, 1, 0)
        ancestor = lookup(0, current)
        suffix_rows.append(jnp.where(ancestor == my_beam, slot_ok, 0))
        fresh_rows.append(fresh_ok)
    to_mask = lambda parts: jnp.where(jnp.concatenate(parts, axis=0) > 0, 0.0, NEG)
    return to_mask(suffix_rows), to_mask(fresh_rows)


def kernel(
    n,
    x_ref,
    sk_ref,
    sv_ref,
    table_ref,
    len_ref,
    parents_ref,
    wq_hbm,
    wkv_hbm,
    wo_hbm,
    pk_hbm,
    pv_hbm,
    out_ref,
    xg,
    qg,
    kvg,
    wq,
    wkv,
    wo,
    pk,
    pv,
    ske,
    sve,
    scores,
    fresh,
    maxes,
    max_in,
    acc,
    acc_in,
    y,
    y_in,
    proj_q,
    proj_kv,
    mask_buf,
    load_sem,
    send_sem,
    recv_sem,
):
    outers = n // 4
    me = lax.axis_index("head")
    outer_id, mid_id, inner_id = me // 4, (me // 2) % 2, me % 2

    def block(d, e, f):
        high = 0
        for i in range(outers.bit_length() - 1):
            high = high + ((outer_id // (1 << i)) % 2 + (d // (1 << i)) % 2) % 2 * (1 << i)
        return high * 4 + (mid_id + e) % 2 * 2 + (inner_id + f) % 2

    tokens, dl = x_ref.shape
    width_q = wq.shape[1]
    width_kv = wkv.shape[1]
    hd = 128
    hq = width_q // hd
    rows = hq * tokens
    own_rows, slots = sk_ref.shape[0], sk_ref.shape[1]
    kv_heads = pk.shape[1] // hd
    group_size = hq * n // kv_heads
    pre = pk.shape[0]
    scale = 1.0 / math.sqrt(hd)
    first_kv = me * own_rows % kv_heads
    blocks = -(-rows // 128)
    f32, bf16 = jnp.float32, jnp.bfloat16

    loads = [
        pltpu.make_async_copy(src, dst, load_sem.at[i])
        for i, (src, dst) in enumerate(
            ((wq_hbm, wq), (wkv_hbm, wkv), (pk_hbm, pk), (pv_hbm, pv), (wo_hbm, wo))
        )
    ]
    for load in loads:
        load.start()

    barrier = pltpu.get_barrier_semaphore()

    def greet(device):
        pl.semaphore_signal(
            barrier, inc=1, device_id={"head": device}, device_id_type=pl.DeviceIdType.MESH
        )

    for e, f in ((0, 1), (1, 0), (1, 1)):
        greet(block(0, e, f))
    for d in range(1, outers):
        greet(block(d, 0, 0))

    xg[me] = x_ref[...]
    for r in range(own_rows):
        zeros = jnp.zeros((hd - slots, hd), bf16)
        ske[r, :slots] = sk_ref[r]
        ske[r, slots:] = zeros
        sve[r, :slots] = sv_ref[r]
        sve[r, slots:] = zeros
    proj_q[...] = jnp.zeros_like(proj_q)
    proj_kv[...] = jnp.zeros_like(proj_kv)
    pl.semaphore_wait(barrier, outers + 2)

    def message(src, dst, phase, slot, device):
        return pltpu.make_async_remote_copy(
            src_ref=src,
            dst_ref=dst,
            send_sem=send_sem.at[phase, slot],
            recv_sem=recv_sem.at[phase, slot],
            device_id={"head": device},
            device_id_type=pl.DeviceIdType.MESH,
        )

    def each(start, stop, body):
        def run(i, carry):
            body(i)
            return carry

        lax.fori_loop(start, stop, run, 0)

    def gather(bufs, phases, use):
        def to_outer(d):
            return [message(b.at[me], b.at[me], p, d, block(d, 0, 0)) for b, p in zip(bufs, phases)]

        def to_mid(d):
            j = block(d, 0, 0)
            return [
                message(b.at[j], b.at[j], p, outers + d, block(0, 1, 0))
                for b, p in zip(bufs, phases)
            ]

        def to_inner(d, e):
            j = block(d, e, 0)
            return [
                message(b.at[j], b.at[j], p, (2 + e) * outers + d, block(0, 0, 1))
                for b, p in zip(bufs, phases)
            ]

        def start(copies):
            for copy in copies:
                copy.start()

        def wait_recv(copies):
            for copy in copies:
                copy.wait_recv()

        def wait_send(copies):
            for copy in copies:
                copy.wait_send()

        each(1, outers, lambda d: start(to_outer(d)))
        start(to_mid(0))
        start(to_inner(0, 0))
        yield
        use(me)

        def from_outer(d):
            wait_recv(to_outer(d))
            start(to_mid(d))
            start(to_inner(d, 0))
            use(block(d, 0, 0))

        def from_mid(d):
            wait_recv(to_mid(d))
            start(to_inner(d, 1))
            use(block(d, 1, 0))

        def from_inner(i):
            wait_recv(to_inner(i % outers, i // outers))
            use(block(i % outers, i // outers, 1))

        each(1, outers, from_outer)
        each(0, outers, from_mid)
        each(0, 2 * outers, from_inner)
        each(1, outers, lambda d: wait_send(to_outer(d)))
        each(0, outers, lambda d: wait_send(to_mid(d)))
        each(0, 2 * outers, lambda i: wait_send(to_inner(i % outers, i // outers)))
        yield

    def project(p):
        at = pl.ds(pl.multiple_of(p * dl, dl), dl)
        tile = xg[p]
        proj_q[...] += jnp.dot(tile, wq[at, :], preferred_element_type=f32)
        proj_kv[...] += jnp.dot(tile, wkv[at, :], preferred_element_type=f32)

    steps = gather([xg], [0], project)
    next(steps)
    my_beam = me * own_rows // kv_heads
    suffix_mask, fresh_mask = masks(
        table_ref, len_ref, parents_ref, my_beam, slots, parents_ref.shape[0]
    )
    mask_buf[0] = suffix_mask
    mask_buf[1] = fresh_mask
    loads[0].wait()
    loads[1].wait()
    next(steps)

    for h in range(hq):
        qg[me, h * tokens : (h + 1) * tokens, :] = proj_q[:, h * hd : (h + 1) * hd].astype(bf16)
    kvg[me] = proj_kv[...].astype(bf16)

    row_id = lax.broadcasted_iota(jnp.int32, (rows, 128), 0)
    lane_id = lax.broadcasted_iota(jnp.int32, (rows, 128), 1)
    eye = row_id % 128 == lane_id

    def to_rows(column, fill, reduce):
        spread = jnp.where(eye, jnp.broadcast_to(column, (rows, 128)), fill)
        return [
            reduce(spread[i * 128 : min(rows, (i + 1) * 128)], axis=0, keepdims=True)
            for i in range(blocks)
        ]

    def to_column(parts, fill, reduce):
        return jnp.concatenate(
            [
                reduce(
                    jnp.where(
                        eye[: min(128, rows - i * 128)],
                        jnp.broadcast_to(part, (min(128, rows - i * 128), 128)),
                        fill,
                    ),
                    axis=1,
                    keepdims=True,
                )
                for i, part in enumerate(parts)
            ],
            axis=0,
        )

    def heads_of(p):
        kv = p * hq // group_size
        off = kv - first_kv
        return kv, off

    suffix_mask = jnp.concatenate([mask_buf[0]] * hq, axis=0)

    def clip(off):
        return jnp.minimum(jnp.maximum(off, 0), own_rows - 1)

    def score(p):
        kv, off = heads_of(p)
        q = qg[p]
        keys = pk[:, pl.ds(pl.multiple_of(kv * hd, hd), hd)]
        nt = (((1,), (1,)), ((), ()))
        s = lax.dot_general(q, keys, nt, preferred_element_type=f32) * scale
        scores[p, :, :pre] = s
        hit = jnp.where((off >= 0) & (off < own_rows), 0.0, NEG)
        e = lax.dot_general(q, ske[clip(off)], nt, preferred_element_type=f32) * scale
        e = e + suffix_mask + hit
        scores[p, :, pre:] = e
        m = jnp.maximum(jnp.max(s, axis=1, keepdims=True), jnp.max(e, axis=1, keepdims=True))
        for i, part in enumerate(to_rows(m, NEG, jnp.max)):
            maxes[0, p, i : i + 1, :] = part

    steps = gather([qg, kvg], [1, 2], score)
    next(steps)
    loads[2].wait()
    next(steps)

    own_kv = me * hq // group_size
    pieces = hd // width_kv if width_kv < hd else 1

    def fresh_block(column):
        if width_kv >= hd:
            j = column * hd // width_kv
            return kvg[j]
        j = column * pieces
        return jnp.concatenate([kvg[j + i] for i in range(pieces)], axis=1)

    fresh_keys = fresh_block(own_kv)
    fresh_values = fresh_block(own_kv + kv_heads)
    pad = jnp.zeros((hd - tokens, hd), bf16)
    fresh_keys = jnp.concatenate([fresh_keys, pad], axis=0)
    fresh_values = jnp.concatenate([fresh_values, pad], axis=0)
    f = lax.dot_general(
        qg[me], fresh_keys, (((1,), (1,)), ((), ())), preferred_element_type=f32
    )
    f = f * scale + jnp.concatenate([mask_buf[1]] * hq, axis=0)
    fresh[...] = f
    for i, part in enumerate(to_rows(jnp.max(f, axis=1, keepdims=True), NEG, jnp.max)):
        maxes[0, me, i : i + 1, :] = jnp.maximum(maxes[0, me, i : i + 1, :], part)

    near = [
        message(maxes.at[0], max_in.at[2 * e + f], 3, 2 * e + f, block(0, e, f))
        for e, f in ((0, 1), (1, 0), (1, 1))
    ]
    for copy in near:
        copy.start()
    for copy in near:
        copy.wait()
    maxes[1] = jnp.maximum(jnp.maximum(maxes[0], max_in[1]), jnp.maximum(max_in[2], max_in[3]))
    far = [
        message(maxes.at[1], max_in.at[4 + d], 3, 4 + d, block(d, 0, 0))
        for d in range(1, outers)
    ]
    for copy in far:
        copy.start()
    for copy in far:
        copy.wait()
    top = maxes[1]
    for d in range(1, outers):
        top = jnp.maximum(top, max_in[4 + d])
    maxes[2] = top

    loads[3].wait()

    def largest(p):
        return to_column(
            [maxes[2, p, i : i + 1, :] for i in range(blocks)], NEG, jnp.max
        )

    def put_totals(p, column):
        parts = to_rows(column, 0.0, jnp.sum)
        parts.append(jnp.zeros((8 - blocks, 128), f32))
        acc[p, rows:, :] = jnp.concatenate(parts, axis=0)

    def weigh(p):
        kv, off = heads_of(p)
        w = jnp.exp(scores[p] - largest(p))
        values = pv[:, pl.ds(pl.multiple_of(kv * hd, hd), hd)]
        wb = w.astype(bf16)
        acc[p, :rows, :] = jnp.dot(
            wb[:, :pre], values, preferred_element_type=f32
        ) + jnp.dot(wb[:, pre:], sve[clip(off)], preferred_element_type=f32)
        put_totals(p, jnp.sum(w, axis=1, keepdims=True))

    def scatter_sum(buf, buf_in, phase, fill, own_extra):
        def to_inner(d, e):
            slot = (2 + e) * outers + d
            return message(
                buf.at[block(d, e, 1)], buf_in.at[slot], phase, slot, block(0, 0, 1)
            )

        def to_mid(d):
            slot = outers + d
            return message(buf.at[block(d, 1, 0)], buf_in.at[slot], phase, slot, block(0, 1, 0))

        def to_outer(d):
            return message(buf.at[block(d, 0, 0)], buf_in.at[d], phase, d, block(d, 0, 0))

        def inner(i):
            d, e = outers - 1 - i % outers, 1 - i // outers
            fill(block(d, e, 1))
            to_inner(d, e).start()

        def mid(i):
            d = outers - 1 - i
            p = block(d, 1, 0)
            fill(p)
            to_inner(d, 1).wait_recv()
            buf[p] += buf_in[3 * outers + d]
            to_mid(d).start()

        def outer(i):
            d = outers - 1 - i
            p = block(d, 0, 0)
            to_inner(d, 0).wait_recv()
            to_mid(d).wait_recv()
            buf[p] += buf_in[2 * outers + d] + buf_in[outers + d]
            to_outer(d).start()

        each(0, 2 * outers, inner)
        each(0, outers, mid)
        each(0, outers, lambda i: fill(block(outers - 1 - i, 0, 0)))
        own_extra()
        each(0, outers - 1, outer)
        to_inner(0, 0).wait_recv()
        to_mid(0).wait_recv()
        total = buf[me] + buf_in[2 * outers] + buf_in[outers]
        for d in range(1, outers):
            to_outer(d).wait_recv()
            total = total + buf_in[d]
        each(0, 2 * outers, lambda i: to_inner(i % outers, i // outers).wait_send())
        each(0, outers, lambda d: to_mid(d).wait_send())
        each(1, outers, lambda d: to_outer(d).wait_send())
        return total

    def add_fresh():
        w = jnp.exp(fresh[...] - largest(me))
        acc[me, :rows, :] += jnp.dot(
            w.astype(bf16), fresh_values, preferred_element_type=f32
        )
        parts = to_rows(jnp.sum(w, axis=1, keepdims=True), 0.0, jnp.sum)
        parts.append(jnp.zeros((8 - blocks, 128), f32))
        acc[me, rows:, :] += jnp.concatenate(parts, axis=0)

    total = scatter_sum(acc, acc_in, 4, weigh, add_fresh)
    column = to_column([total[rows + i : rows + i + 1] for i in range(blocks)], 0.0, jnp.sum)
    attended = (total[:rows] / column).astype(bf16)
    attended = jnp.concatenate(
        [attended[h * tokens : (h + 1) * tokens] for h in range(hq)], axis=1
    )
    loads[4].wait()

    def out_block(p):
        columns = wo[:, pl.ds(pl.multiple_of(p * dl, dl), dl)]
        y[p] = jnp.dot(attended, columns, preferred_element_type=f32)

    result = scatter_sum(y, y_in, 5, out_block, lambda: None)
    out_ref[...] = result.astype(bf16)


def local(
    inputs,
    w_query,
    w_keyval,
    w_out,
    prefix_keys,
    prefix_values,
    suffix_keys,
    suffix_values,
    page_table,
    suffix_len,
    parents,
):
    n = lax.axis_size("head")
    steps, beams, dl = inputs.shape
    tokens = steps * beams
    own_rows, slots, hd = suffix_keys.shape
    width_q, width_kv = w_query.shape[1], w_keyval.shape[1]
    rows = width_q // hd * tokens
    blocks = -(-rows // 128)
    pre = prefix_keys.shape[0]
    bf16, f32 = jnp.bfloat16, jnp.float32
    vmem = pl.BlockSpec(memory_space=pltpu.VMEM)
    hbm = pl.BlockSpec(memory_space=pl.ANY)
    out = pl.pallas_call(
        functools.partial(kernel, n),
        out_shape=jax.ShapeDtypeStruct((tokens, dl), bf16),
        in_specs=[vmem] * 6 + [hbm] * 5,
        out_specs=vmem,
        scratch_shapes=[
            pltpu.VMEM((n, tokens, dl), bf16),
            pltpu.VMEM((n, rows, hd), bf16),
            pltpu.VMEM((n, tokens, width_kv), bf16),
            pltpu.VMEM(w_query.shape, bf16),
            pltpu.VMEM(w_keyval.shape, bf16),
            pltpu.VMEM(w_out.shape, bf16),
            pltpu.VMEM(prefix_keys.shape, bf16),
            pltpu.VMEM(prefix_values.shape, bf16),
            pltpu.VMEM((own_rows, hd, hd), bf16),
            pltpu.VMEM((own_rows, hd, hd), bf16),
            pltpu.VMEM((n, rows, pre + hd), f32),
            pltpu.VMEM((rows, hd), f32),
            pltpu.VMEM((3, n, blocks, 128), f32),
            pltpu.VMEM((4 + n // 4, n, blocks, 128), f32),
            pltpu.VMEM((n, rows + 8, hd), f32),
            pltpu.VMEM((n, rows + 8, hd), f32),
            pltpu.VMEM((n, tokens, dl), f32),
            pltpu.VMEM((n, tokens, dl), f32),
            pltpu.VMEM((tokens, width_q), f32),
            pltpu.VMEM((tokens, width_kv), f32),
            pltpu.VMEM((2, tokens, 128), f32),
            pltpu.SemaphoreType.DMA((5,)),
            pltpu.SemaphoreType.DMA((6, n)),
            pltpu.SemaphoreType.DMA((6, n)),
        ],
        compiler_params=pltpu.CompilerParams(
            collective_id=0, has_side_effects=True, vmem_limit_bytes=56 * 1024 * 1024
        ),
    )(
        inputs.reshape(tokens, dl),
        suffix_keys,
        suffix_values,
        page_table,
        suffix_len.reshape(1, -1),
        parents,
        w_query,
        w_keyval,
        w_out,
        prefix_keys,
        prefix_values,
    )
    return out.reshape(steps, beams, dl)


def solution(mesh):
    return jax.shard_map(
        local,
        mesh=mesh,
        in_specs=(
            P("groups", None, "head"),
            P(None, "head"),
            P(None, "head"),
            P("head", None),
            P(("groups", "head"), None),
            P(("groups", "head"), None),
            P(("groups", "head"), None, None),
            P(("groups", "head"), None, None),
            P("groups", None),
            P("groups"),
            P("groups", None),
        ),
        out_specs=P("groups", None, "head"),
        check_vma=False,
    )
```

```python
import functools
import math

import jax
import jax.numpy as jnp
from jax import lax
from jax.experimental import pallas as pl
from jax.experimental.pallas import tpu as pltpu
from jax.sharding import PartitionSpec as P

NEG = float("-inf")


def masks(table_ref, len_ref, parents_ref, my_beam, slots, steps):
    i32 = jnp.int32
    page_count, beams = table_ref.shape
    page_size = slots // page_count
    lane = lax.broadcasted_iota(i32, (beams, 128), 1)
    beam_lane = lax.broadcasted_iota(i32, (1, beams), 1)
    page_of = jnp.zeros((beams, 128), i32)
    for page in range(1, page_count):
        page_of = page_of + jnp.where(lane >= page * page_size, 1, 0)
    logical = jnp.zeros((beams, 128), i32)
    for page in range(1, page_count):
        physical = jnp.sum(
            jnp.where(beam_lane == my_beam, table_ref[page : page + 1, :], 0),
            axis=1,
            keepdims=True,
        )
        logical = logical + jnp.where(page_of == physical, page, 0)
    own_len = jnp.sum(
        jnp.where(beam_lane == my_beam, len_ref[...], 0), axis=1, keepdims=True
    )
    place = logical * page_size + lane - page_of * page_size
    slot_ok = jnp.where((place < own_len) & (lane < slots), 1, 0)
    square_lane = lax.broadcasted_iota(i32, (beams, beams), 1)
    square_row = lax.broadcasted_iota(i32, (beams, beams), 0)

    def lookup(step, column):
        table = jnp.broadcast_to(parents_ref[step : step + 1, :], (beams, beams))
        return jnp.sum(jnp.where(square_lane == column, table, 0), axis=1, keepdims=True)

    first = jnp.sum(jnp.where(square_lane == square_row, square_lane, 0), axis=1, keepdims=True)
    suffix_rows, fresh_rows = [], []
    for step in range(steps):
        current = first
        fresh_ok = jnp.where(lane == current + step * beams, 1, 0)
        for later in range(step, 0, -1):
            current = lookup(later, current)
            fresh_ok = fresh_ok + jnp.where(lane == current + (later - 1) * beams, 1, 0)
        ancestor = lookup(0, current)
        suffix_rows.append(jnp.where(ancestor == my_beam, slot_ok, 0))
        fresh_rows.append(fresh_ok)
    to_mask = lambda parts: jnp.where(jnp.concatenate(parts, axis=0) > 0, 0.0, NEG)
    return to_mask(suffix_rows), to_mask(fresh_rows)


def kernel(
    n,
    x_ref,
    sk_ref,
    sv_ref,
    table_ref,
    len_ref,
    parents_ref,
    wq_hbm,
    wkv_hbm,
    wo_hbm,
    pk_hbm,
    pv_hbm,
    out_ref,
    xg,
    qg,
    kvg,
    wq,
    wkv,
    wo,
    pk,
    pv,
    ske,
    sve,
    scores,
    fresh,
    maxes,
    max_in,
    acc,
    acc_in,
    y,
    y_in,
    proj_q,
    proj_kv,
    mask_buf,
    load_sem,
    send_sem,
    recv_sem,
):
    outers = n // 4
    me = lax.axis_index("head")
    outer_id, mid_id, inner_id = me // 4, (me // 2) % 2, me % 2

    def block(d, e, f):
        high = 0
        for i in range(outers.bit_length() - 1):
            high = high + ((outer_id // (1 << i)) % 2 + (d // (1 << i)) % 2) % 2 * (1 << i)
        return high * 4 + (mid_id + e) % 2 * 2 + (inner_id + f) % 2

    tokens, dl = x_ref.shape
    width_q = wq.shape[1]
    width_kv = wkv.shape[1]
    hd = 128
    hq = width_q // hd
    rows = hq * tokens
    own_rows, slots = sk_ref.shape[0], sk_ref.shape[1]
    kv_heads = pk.shape[1] // hd
    group_size = hq * n // kv_heads
    pre = pk.shape[0]
    scale = 1.0 / math.sqrt(hd)
    first_kv = me * own_rows % kv_heads
    blocks = -(-rows // 128)
    f32, bf16 = jnp.float32, jnp.bfloat16

    loads = [
        pltpu.make_async_copy(src, dst, load_sem.at[i])
        for i, (src, dst) in enumerate(
            ((wq_hbm, wq), (wkv_hbm, wkv), (pk_hbm, pk), (pv_hbm, pv), (wo_hbm, wo))
        )
    ]
    for load in loads[:2]:
        load.start()

    barrier = pltpu.get_barrier_semaphore()

    def greet(device):
        pl.semaphore_signal(
            barrier, inc=1, device_id={"head": device}, device_id_type=pl.DeviceIdType.MESH
        )

    for e, f in ((0, 1), (1, 0), (1, 1)):
        greet(block(0, e, f))
    for d in range(1, outers):
        greet(block(d, 0, 0))

    xg[me] = x_ref[...]
    for r in range(own_rows):
        zeros = jnp.zeros((hd - slots, hd), bf16)
        ske[r, :slots] = sk_ref[r]
        ske[r, slots:] = zeros
        sve[r, :slots] = sv_ref[r]
        sve[r, slots:] = zeros
    proj_q[...] = jnp.zeros_like(proj_q)
    proj_kv[...] = jnp.zeros_like(proj_kv)
    pl.semaphore_wait(barrier, outers + 2)

    def message(src, dst, phase, slot, device):
        return pltpu.make_async_remote_copy(
            src_ref=src,
            dst_ref=dst,
            send_sem=send_sem.at[phase, slot],
            recv_sem=recv_sem.at[phase, slot],
            device_id={"head": device},
            device_id_type=pl.DeviceIdType.MESH,
        )

    def each(start, stop, body):
        def run(i, carry):
            body(i)
            return carry

        lax.fori_loop(start, stop, run, 0)

    def gather(bufs, phases, use):
        def to_outer(d):
            return [message(b.at[me], b.at[me], p, d, block(d, 0, 0)) for b, p in zip(bufs, phases)]

        def to_mid(d):
            j = block(d, 0, 0)
            return [
                message(b.at[j], b.at[j], p, outers + d, block(0, 1, 0))
                for b, p in zip(bufs, phases)
            ]

        def to_inner(d, e):
            j = block(d, e, 0)
            return [
                message(b.at[j], b.at[j], p, (2 + e) * outers + d, block(0, 0, 1))
                for b, p in zip(bufs, phases)
            ]

        def start(copies):
            for copy in copies:
                copy.start()

        def wait_recv(copies):
            for copy in copies:
                copy.wait_recv()

        def wait_send(copies):
            for copy in copies:
                copy.wait_send()

        each(1, outers, lambda d: start(to_outer(d)))
        start(to_mid(0))
        start(to_inner(0, 0))
        yield
        use(me)

        def from_outer(d):
            wait_recv(to_outer(d))
            start(to_mid(d))
            start(to_inner(d, 0))
            use(block(d, 0, 0))

        def from_mid(d):
            wait_recv(to_mid(d))
            start(to_inner(d, 1))
            use(block(d, 1, 0))

        def from_inner(i):
            wait_recv(to_inner(i % outers, i // outers))
            use(block(i % outers, i // outers, 1))

        each(1, outers, from_outer)
        each(0, outers, from_mid)
        each(0, 2 * outers, from_inner)
        each(1, outers, lambda d: wait_send(to_outer(d)))
        each(0, outers, lambda d: wait_send(to_mid(d)))
        each(0, 2 * outers, lambda i: wait_send(to_inner(i % outers, i // outers)))
        yield

    def project(p):
        at = pl.ds(pl.multiple_of(p * dl, dl), dl)
        tile = xg[p]
        proj_q[...] += jnp.dot(tile, wq[at, :], preferred_element_type=f32)
        proj_kv[...] += jnp.dot(tile, wkv[at, :], preferred_element_type=f32)

    steps = gather([xg], [0], project)
    next(steps)
    my_beam = me * own_rows // kv_heads
    suffix_mask, fresh_mask = masks(
        table_ref, len_ref, parents_ref, my_beam, slots, parents_ref.shape[0]
    )
    mask_buf[0] = suffix_mask
    mask_buf[1] = fresh_mask
    loads[0].wait()
    loads[1].wait()
    for load in loads[2:]:
        load.start()
    next(steps)

    for h in range(hq):
        qg[me, h * tokens : (h + 1) * tokens, :] = proj_q[:, h * hd : (h + 1) * hd].astype(bf16)
    kvg[me] = proj_kv[...].astype(bf16)

    row_id = lax.broadcasted_iota(jnp.int32, (rows, 128), 0)
    lane_id = lax.broadcasted_iota(jnp.int32, (rows, 128), 1)
    eye = row_id % 128 == lane_id

    def to_rows(column, fill, reduce):
        spread = jnp.where(eye, jnp.broadcast_to(column, (rows, 128)), fill)
        return [
            reduce(spread[i * 128 : min(rows, (i + 1) * 128)], axis=0, keepdims=True)
            for i in range(blocks)
        ]

    def to_column(parts, fill, reduce):
        return jnp.concatenate(
            [
                reduce(
                    jnp.where(
                        eye[: min(128, rows - i * 128)],
                        jnp.broadcast_to(part, (min(128, rows - i * 128), 128)),
                        fill,
                    ),
                    axis=1,
                    keepdims=True,
                )
                for i, part in enumerate(parts)
            ],
            axis=0,
        )

    def heads_of(p):
        kv = p * hq // group_size
        off = kv - first_kv
        return kv, off

    suffix_mask = jnp.concatenate([mask_buf[0]] * hq, axis=0)

    def clip(off):
        return jnp.minimum(jnp.maximum(off, 0), own_rows - 1)

    def score(p):
        kv, off = heads_of(p)
        q = qg[p]
        keys = pk[:, pl.ds(pl.multiple_of(kv * hd, hd), hd)]
        nt = (((1,), (1,)), ((), ()))
        s = lax.dot_general(q, keys, nt, preferred_element_type=f32) * scale
        scores[p, :, :pre] = s
        hit = jnp.where((off >= 0) & (off < own_rows), 0.0, NEG)
        e = lax.dot_general(q, ske[clip(off)], nt, preferred_element_type=f32) * scale
        e = e + suffix_mask + hit
        scores[p, :, pre:] = e
        m = jnp.maximum(jnp.max(s, axis=1, keepdims=True), jnp.max(e, axis=1, keepdims=True))
        for i, part in enumerate(to_rows(m, NEG, jnp.max)):
            maxes[0, p, i : i + 1, :] = part

    steps = gather([qg, kvg], [1, 2], score)
    next(steps)
    loads[2].wait()
    next(steps)

    own_kv = me * hq // group_size
    pieces = hd // width_kv if width_kv < hd else 1

    def fresh_block(column):
        if width_kv >= hd:
            j = column * hd // width_kv
            return kvg[j]
        j = column * pieces
        return jnp.concatenate([kvg[j + i] for i in range(pieces)], axis=1)

    fresh_keys = fresh_block(own_kv)
    fresh_values = fresh_block(own_kv + kv_heads)
    pad = jnp.zeros((hd - tokens, hd), bf16)
    fresh_keys = jnp.concatenate([fresh_keys, pad], axis=0)
    fresh_values = jnp.concatenate([fresh_values, pad], axis=0)
    f = lax.dot_general(
        qg[me], fresh_keys, (((1,), (1,)), ((), ())), preferred_element_type=f32
    )
    f = f * scale + jnp.concatenate([mask_buf[1]] * hq, axis=0)
    fresh[...] = f
    for i, part in enumerate(to_rows(jnp.max(f, axis=1, keepdims=True), NEG, jnp.max)):
        maxes[0, me, i : i + 1, :] = jnp.maximum(maxes[0, me, i : i + 1, :], part)

    def put_totals(p, column):
        parts = to_rows(column, 0.0, jnp.sum)
        parts.append(jnp.zeros((8 - blocks, 128), f32))
        acc[p, rows:, :] = jnp.concatenate(parts, axis=0)

    def soften(p):
        own = to_column([maxes[0, p, i : i + 1, :] for i in range(blocks)], NEG, jnp.max)
        w = jnp.exp(scores[p] - own)
        scores[p] = w
        put_totals(p, jnp.sum(w, axis=1, keepdims=True))

    near = [
        message(maxes.at[0], max_in.at[2 * e + f], 3, 2 * e + f, block(0, e, f))
        for e, f in ((0, 1), (1, 0), (1, 1))
    ]
    for copy in near:
        copy.start()
    each(0, n // 2, soften)
    for copy in near:
        copy.wait()
    maxes[1] = jnp.maximum(jnp.maximum(maxes[0], max_in[1]), jnp.maximum(max_in[2], max_in[3]))
    far = [
        message(maxes.at[1], max_in.at[4 + d], 3, 4 + d, block(d, 0, 0))
        for d in range(1, outers)
    ]
    for copy in far:
        copy.start()
    each(n // 2, n, soften)
    for copy in far:
        copy.wait()
    top = maxes[1]
    for d in range(1, outers):
        top = jnp.maximum(top, max_in[4 + d])
    maxes[2] = top
    maxes[1] = jnp.exp(maxes[0] - top)

    loads[3].wait()

    def largest(p):
        return to_column(
            [maxes[2, p, i : i + 1, :] for i in range(blocks)], NEG, jnp.max
        )

    def weigh(p):
        kv, off = heads_of(p)
        factor = [maxes[1, p, i : i + 1, :] for i in range(blocks)]
        w = scores[p] * to_column(factor, 0.0, jnp.sum)
        values = pv[:, pl.ds(pl.multiple_of(kv * hd, hd), hd)]
        wb = w.astype(bf16)
        acc[p, :rows, :] = jnp.dot(
            wb[:, :pre], values, preferred_element_type=f32
        ) + jnp.dot(wb[:, pre:], sve[clip(off)], preferred_element_type=f32)
        for i in range(blocks):
            acc[p, rows + i : rows + i + 1, :] *= jnp.where(
                lane_id[:1] < rows - i * 128, factor[i], 0.0
            )

    def scatter_sum(buf, buf_in, phase, fill, own_extra):
        def to_inner(d, e):
            slot = (2 + e) * outers + d
            return message(
                buf.at[block(d, e, 1)], buf_in.at[slot], phase, slot, block(0, 0, 1)
            )

        def to_mid(d):
            slot = outers + d
            return message(buf.at[block(d, 1, 0)], buf_in.at[slot], phase, slot, block(0, 1, 0))

        def to_outer(d):
            return message(buf.at[block(d, 0, 0)], buf_in.at[d], phase, d, block(d, 0, 0))

        def inner(d, e):
            fill(block(d, e, 1))
            to_inner(d, e).start()
            fill(block(d, e, 0))

        def mid(d):
            p = block(d, 1, 0)
            to_inner(d, 1).wait_recv()
            buf[p] += buf_in[3 * outers + d]
            to_mid(d).start()

        def first(i):
            d = outers - 1 - i
            inner(d, 1)
            mid(d + 1)

        def outer(i):
            d = outers - 1 - i
            p = block(d, 0, 0)
            to_inner(d, 0).wait_recv()
            to_mid(d).wait_recv()
            buf[p] += buf_in[2 * outers + d] + buf_in[outers + d]
            to_outer(d).start()

        inner(outers - 1, 1)
        each(1, outers, first)
        inner(outers - 1, 0)
        mid(0)
        each(1, outers, lambda i: inner(outers - 1 - i, 0))
        own_extra()
        each(0, outers - 1, outer)
        to_inner(0, 0).wait_recv()
        to_mid(0).wait_recv()
        total = buf[me] + buf_in[2 * outers] + buf_in[outers]
        for d in range(1, outers):
            to_outer(d).wait_recv()
            total = total + buf_in[d]
        each(0, 2 * outers, lambda i: to_inner(i % outers, i // outers).wait_send())
        each(0, outers, lambda d: to_mid(d).wait_send())
        each(1, outers, lambda d: to_outer(d).wait_send())
        return total

    def add_fresh():
        w = jnp.exp(fresh[...] - largest(me))
        acc[me, :rows, :] += jnp.dot(
            w.astype(bf16), fresh_values, preferred_element_type=f32
        )
        parts = to_rows(jnp.sum(w, axis=1, keepdims=True), 0.0, jnp.sum)
        parts.append(jnp.zeros((8 - blocks, 128), f32))
        acc[me, rows:, :] += jnp.concatenate(parts, axis=0)

    total = scatter_sum(acc, acc_in, 4, weigh, add_fresh)
    column = to_column([total[rows + i : rows + i + 1] for i in range(blocks)], 0.0, jnp.sum)
    attended = (total[:rows] / column).astype(bf16)
    attended = jnp.concatenate(
        [attended[h * tokens : (h + 1) * tokens] for h in range(hq)], axis=1
    )
    loads[4].wait()

    def out_block(p):
        columns = wo[:, pl.ds(pl.multiple_of(p * dl, dl), dl)]
        y[p] = jnp.dot(attended, columns, preferred_element_type=f32)

    result = scatter_sum(y, y_in, 5, out_block, lambda: None)
    out_ref[...] = result.astype(bf16)


def local(
    inputs,
    w_query,
    w_keyval,
    w_out,
    prefix_keys,
    prefix_values,
    suffix_keys,
    suffix_values,
    page_table,
    suffix_len,
    parents,
):
    n = lax.axis_size("head")
    steps, beams, dl = inputs.shape
    tokens = steps * beams
    own_rows, slots, hd = suffix_keys.shape
    width_q, width_kv = w_query.shape[1], w_keyval.shape[1]
    rows = width_q // hd * tokens
    blocks = -(-rows // 128)
    pre = prefix_keys.shape[0]
    bf16, f32 = jnp.bfloat16, jnp.float32
    vmem = pl.BlockSpec(memory_space=pltpu.VMEM)
    hbm = pl.BlockSpec(memory_space=pl.ANY)
    out = pl.pallas_call(
        functools.partial(kernel, n),
        out_shape=jax.ShapeDtypeStruct((tokens, dl), bf16),
        in_specs=[vmem] * 6 + [hbm] * 5,
        out_specs=vmem,
        scratch_shapes=[
            pltpu.VMEM((n, tokens, dl), bf16),
            pltpu.VMEM((n, rows, hd), bf16),
            pltpu.VMEM((n, tokens, width_kv), bf16),
            pltpu.VMEM(w_query.shape, bf16),
            pltpu.VMEM(w_keyval.shape, bf16),
            pltpu.VMEM(w_out.shape, bf16),
            pltpu.VMEM(prefix_keys.shape, bf16),
            pltpu.VMEM(prefix_values.shape, bf16),
            pltpu.VMEM((own_rows, hd, hd), bf16),
            pltpu.VMEM((own_rows, hd, hd), bf16),
            pltpu.VMEM((n, rows, pre + hd), f32),
            pltpu.VMEM((rows, hd), f32),
            pltpu.VMEM((3, n, blocks, 128), f32),
            pltpu.VMEM((4 + n // 4, n, blocks, 128), f32),
            pltpu.VMEM((n, rows + 8, hd), f32),
            pltpu.VMEM((n, rows + 8, hd), f32),
            pltpu.VMEM((n, tokens, dl), f32),
            pltpu.VMEM((n, tokens, dl), f32),
            pltpu.VMEM((tokens, width_q), f32),
            pltpu.VMEM((tokens, width_kv), f32),
            pltpu.VMEM((2, tokens, 128), f32),
            pltpu.SemaphoreType.DMA((5,)),
            pltpu.SemaphoreType.DMA((6, n)),
            pltpu.SemaphoreType.DMA((6, n)),
        ],
        compiler_params=pltpu.CompilerParams(
            collective_id=0, has_side_effects=True, vmem_limit_bytes=56 * 1024 * 1024
        ),
    )(
        inputs.reshape(tokens, dl),
        suffix_keys,
        suffix_values,
        page_table.T,
        suffix_len.reshape(1, -1),
        parents,
        w_query,
        w_keyval,
        w_out,
        prefix_keys,
        prefix_values,
    )
    return out.reshape(steps, beams, dl)


def solution(mesh):
    return jax.shard_map(
        local,
        mesh=mesh,
        in_specs=(
            P("groups", None, "head"),
            P(None, "head"),
            P(None, "head"),
            P("head", None),
            P(("groups", "head"), None),
            P(("groups", "head"), None),
            P(("groups", "head"), None, None),
            P(("groups", "head"), None, None),
            P("groups", None),
            P("groups"),
            P("groups", None),
        ),
        out_specs=P("groups", None, "head"),
        check_vma=False,
    )
```
